32 devices in a mesh: cell: 8 (over y, x, core), gene: 4 (over z).
Axes of the slice: x: 2, y: 2, z: 4, core: 2. Of those that a mesh axis runs over, the one named last changes fastest.
Arguments:
- counts: bfloat16 [16384, 4096], P('cell', 'gene'), may hold values from -14 to 14
- loadings: bfloat16 [4096, 256], P('gene'), may hold values from -0.09375 to 0.09375
- kernel_widths: float32 [8], replicated, may hold values from 0.4 to 1.6
- width_index: int32 [16384], P(('cell', 'gene')), may hold values from 0 to 7
- block_fill: int32 [8], replicated, may hold values from 1 to 2048, 12288 in all
- plan: int32 [2], replicated, may hold values from 1 to 7, as said below
Outputs:
- density: float32 [16384], P(('cell', 'gene'))
- eccentricity: float32 [16384], P(('cell', 'gene'))
The draws below stay inside these ranges and needn't reach their ends.
Inputs may be any that keep to these rules, and one draw needn't show every extreme that they name: `plan`: the 2 values are distinct and one of them is 7.
All inputs are finite; a program needn't handle non-finite values.
Results may differ from the reference program's by a relative error of at most 0.00031.
Values may be sent and summed in bfloat16 or wider, within the bound.
A program may use at most 64 MiB of HBM per device.

```python
import math
import jax
import jax.numpy as jnp
import numpy as np
from jax import lax

G = 4096
PC = 256
NWIDTH = 8
ROUNDS = 2
BLK = 2048
NBLOCKS = 8
CELLS = 16384


def draw_counts(key, part):
    key = jax.random.fold_in(key, 11)
    key_centre, key_label, key_noise, key_scale = jax.random.split(key, 4)
    centres = jnp.clip(jax.random.normal(key_centre, (48, G), jnp.float32), -4.0, 4.0)
    labels = jax.random.randint(key_label, (CELLS,), 0, 48).astype(jnp.int32)
    noise_scale = jnp.exp(jax.random.uniform(key_scale, (CELLS, 1), jnp.float32, jnp.log(0.25), jnp.log(0.75)))
    amplitude = jnp.full((48, 1), 2.0, jnp.float32)
    noise = jnp.clip(jax.random.normal(key_noise, (CELLS, G), jnp.float32), -4.0, 4.0)
    placed = (centres * amplitude)[labels]
    return (placed + noise_scale * noise).astype(jnp.bfloat16)


def draw_plan(key, part):
    key = jax.random.fold_in(key, 7)
    first, second = jax.random.split(key)
    other = jax.random.randint(first, (1,), 1, NBLOCKS - 1).astype(jnp.int32)
    far = jnp.full((1,), NBLOCKS - 1, jnp.int32)
    flip = jax.random.randint(second, (), 0, 2)
    return jnp.where(flip == 1, jnp.concatenate([far, other]), jnp.concatenate([other, far])).astype(jnp.int32)


def with_ends(entries, stream_key, least, top_value):
    index_at = [jax.random.randint(jax.random.fold_in(stream_key, axis), (), 0, length) for axis, length in enumerate(entries.shape)]
    main_axis = entries.shape.index(max(entries.shape))
    neighbour = index_at[:main_axis] + [(index_at[main_axis] + 1) % entries.shape[main_axis]] + index_at[main_axis + 1:]
    return entries.at[tuple(index_at)].set(least).at[tuple(neighbour)].set(top_value)


def levels(stream_key, shape, pieces, least, largest):
    factor_of = 1.0
    for position, parts in pieces:
        heights = jax.random.uniform(jax.random.fold_in(jax.random.fold_in(stream_key, 6), position), (parts,), jnp.float32, least / len(pieces), largest / len(pieces))
        factor_of = factor_of * jnp.repeat(jnp.exp(heights), shape[position] // parts).reshape((-1,) + (1,) * (len(shape) - 1 - position))
    return factor_of


def profile(amount, total, bound, slope):
    loads = [(1 << 20) // math.isqrt(rank ** slope) + 1 for rank in range(2, amount + 1)]
    rest, holding = total - bound - (amount - 1), [1] * (amount - 1)
    while rest > 0:
        free = [i for i in range(amount - 1) if holding[i] < bound]
        pool, budget = sum([loads[i] for i in free]), rest
        for i in free:
            addition = min(bound - holding[i], max(1, budget * loads[i] // pool), rest)
            holding[i] = holding[i] + addition
            rest = rest - addition
    return np.array([bound] + holding)


def ragged_sizes(stream_key, number_of, total, bound, lean):
    if number_of == 2:
        one = jax.random.randint(stream_key, (), max(1, total - bound), min(bound, total - 1) + 1)
        return jnp.stack([one, total - one])
    sizes = jnp.asarray(profile(number_of, total, bound, lean), jnp.int32)
    twos = (number_of - 1) // 2
    donor, receiver = sizes[1:1 + 2 * twos:2], sizes[2:2 + 2 * twos:2]
    margin = jnp.minimum(donor - 1, bound - receiver)
    passed = jax.random.randint(jax.random.fold_in(stream_key, 1), (twos,), 0, 1 << 20) % (margin + 1)
    sizes = sizes.at[1:1 + 2 * twos:2].set(donor - passed).at[2:2 + 2 * twos:2].set(receiver + passed)
    return sizes[jax.random.permutation(jax.random.fold_in(stream_key, 2), number_of)]


def normal_values(own_key, extent, scale, limit, pieces=(), held_as=jnp.bfloat16):
    loudness = levels(own_key, extent, pieces, -0.22, 0.18) if pieces else 1.0
    array = jax.random.normal(own_key, extent, jnp.float32) * scale * loudness
    return jnp.minimum(jnp.maximum(array, -limit), limit).astype(held_as)


def setup_inputs(seed: int = 0) -> dict:
    splits = jax.random.split(jax.random.key(seed), 7)
    return {
        "counts": draw_counts(jax.random.fold_in(splits[6], 71), 0),
        "loadings": normal_values(splits[1], (G, PC), G ** -0.5, 0.09375, ((0, 4),)),
        "kernel_widths": jnp.clip(jnp.exp(jax.random.uniform(splits[2], (NWIDTH,), jnp.float32, math.log(0.4), math.log(1.6))), 0.4, 1.6),
        "width_index": with_ends(jax.random.randint(splits[3], (CELLS,), 0, NWIDTH), jax.random.fold_in(splits[3], 1), 0, NWIDTH - 1).astype(jnp.int32),
        "block_fill": ragged_sizes(splits[4], NBLOCKS, NBLOCKS * BLK * 3 // 4, BLK, 1).astype(jnp.int32),
        "plan": draw_plan(jax.random.fold_in(splits[6], 71), 0),
    }


def block_terms(queries, coef, keys, fill):
    qf = queries.astype(jnp.float32)
    kf = keys.astype(jnp.float32)
    qnorm = lax.optimization_barrier(jnp.sum(qf * qf, axis=1))
    knorm = lax.optimization_barrier(jnp.sum(kf * kf, axis=1))
    inner = jnp.einsum('qc,kc->qk', qf, kf, precision=lax.Precision.HIGHEST)
    dist = jnp.maximum(qnorm[:, None] + knorm[None, :] - 2.0 * inner, 0.0)
    live = jnp.arange(keys.shape[0], dtype=jnp.int32)[None, :] < fill
    kernel = jnp.where(live, jnp.exp(-dist * coef[:, None]), 0.0)
    return (lax.optimization_barrier(jnp.sum(kernel, axis=1)), lax.optimization_barrier(jnp.max(jnp.where(live, dist, 0.0), axis=1)))

def reference(counts, loadings, kernel_widths, width_index, block_fill, plan):
    scores = jnp.dot(counts, loadings, preferred_element_type=jnp.float32).astype(jnp.bfloat16)
    blocks = scores.reshape(NBLOCKS, BLK, PC)
    picked = width_index[:, None] == jnp.arange(NWIDTH, dtype=jnp.int32)[None, :]
    width = lax.optimization_barrier(jnp.sum(jnp.where(picked, kernel_widths[None, :], 0.0), axis=1))
    coef = (1.0 / (2.0 * PC * width * width)).reshape(NBLOCKS, BLK)

    def one_block(index):
        queries = blocks[index]
        total, top = block_terms(queries, coef[index], queries, block_fill[index])
        for step in range(ROUNDS):
            other = jnp.bitwise_xor(index, plan[step]).astype(jnp.int32)
            more, far = block_terms(queries, coef[index], blocks[other], block_fill[other])
            total = total + more
            top = jnp.maximum(top, far)
        qlive = jnp.arange(BLK, dtype=jnp.int32) < block_fill[index]
        density = jnp.where(qlive, jnp.log(total), 0.0)
        spread = jnp.where(qlive, jnp.sqrt(top / PC), 0.0)
        return (density, spread)
    density, spread = lax.map(one_block, jnp.arange(NBLOCKS, dtype=jnp.int32))
    return (density.reshape(CELLS), spread.reshape(CELLS))
```

```python
import jax
import jax.numpy as jnp
from jax import lax
from jax.sharding import PartitionSpec as P


def exchange(value, stride, axis):
    cells = lax.axis_size(axis)
    for bit in range(cells.bit_length() - 1):
        pairs = [(source, source ^ (1 << bit)) for source in range(cells)]
        chosen = jnp.bitwise_and(jnp.right_shift(stride, bit), 1) == 1
        value = lax.cond(
            chosen,
            lambda v: jax.tree.map(lambda a: lax.ppermute(a, axis, pairs), v),
            lambda v: v,
            value,
        )
    return value


def block_terms(queries, coef, keys, fill):
    qf = queries.astype(jnp.float32)
    kf = keys.astype(jnp.float32)
    qnorm = jnp.sum(qf * qf, axis=1)
    knorm = jnp.sum(kf * kf, axis=1)
    inner = jnp.einsum("qc,kc->qk", queries, keys, preferred_element_type=jnp.float32)
    dist = jnp.maximum(qnorm[:, None] + knorm[None, :] - 2.0 * inner, 0.0)
    live = jnp.arange(keys.shape[0], dtype=jnp.int32)[None, :] < fill
    kernel = jnp.where(live, jnp.exp(-dist * coef[:, None]), 0.0)
    return (jnp.sum(kernel, axis=1), jnp.max(jnp.where(live, dist, 0.0), axis=1))


def lookup(table, index):
    slots = jnp.arange(table.shape[0], dtype=jnp.int32)
    return jnp.sum(jnp.where(slots == index, table, 0))


def by_exchange(counts, loadings, kernel_widths, width_index, block_fill, plan):
    groups = lax.axis_size("gene")
    share = counts.shape[0] // groups
    gene_pos = lax.axis_index("gene")
    own_fill = lookup(block_fill, lax.axis_index("cell"))
    partial_scores = jnp.dot(counts, loadings, preferred_element_type=jnp.float32)
    mine = lax.psum_scatter(partial_scores, "gene", scatter_dimension=0, tiled=True)
    mine = mine.astype(jnp.bfloat16)
    whole = lax.all_gather(mine, "gene", axis=0, tiled=True)
    comps = whole.shape[1]
    picked = width_index[:, None] == jnp.arange(kernel_widths.shape[0], dtype=jnp.int32)[None, :]
    width = jnp.sum(jnp.where(picked, kernel_widths[None, :], 0.0), axis=1)
    coef = 1.0 / (2.0 * comps * width * width)
    total, top = block_terms(mine, coef, whole, own_fill)
    for step in range(plan.shape[0]):
        guests, guest_coef = exchange((mine, coef), plan[step], "cell")
        terms = block_terms(guests, guest_coef, whole, own_fill)
        more, far = exchange(terms, plan[step], "cell")
        total = total + more
        top = jnp.maximum(top, far)
    positions = gene_pos * share + jnp.arange(share, dtype=jnp.int32)
    qlive = positions < own_fill
    density = jnp.where(qlive, jnp.log(total), 0.0)
    spread = jnp.where(qlive, jnp.sqrt(top / comps), 0.0)
    return (density, spread)


def solution(mesh):
    placed = (P("cell", "gene"), P("gene", None), P(), P(("cell", "gene")), P(), P())
    return jax.shard_map(
        by_exchange,
        mesh=mesh,
        in_specs=placed,
        out_specs=(P(("cell", "gene")), P(("cell", "gene"))),
        check_vma=False,
    )
```

```python
import functools
import math
import jax
import jax.numpy as jnp
from jax import lax
from jax.experimental import pallas as pl
from jax.experimental.pallas import tpu as pltpu
from jax.sharding import PartitionSpec as P

MESH = pl.DeviceIdType.MESH
PIECE = 128
TILE = 256
FAR = 1e30


def flip(place, mask):
    for bit in range(mask.bit_length()):
        if (mask >> bit) & 1:
            place = place + (1 << bit) * (1 - 2 * (place // (1 << bit) % 2))
    return place


def remote(src, dst, send, recv, **device):
    return pltpu.make_async_remote_copy(
        src_ref=src, dst_ref=dst, send_sem=send, recv_sem=recv, device_id=device, device_id_type=MESH
    )


def kernel(
    cells,
    counts,
    loadings,
    index,
    widths,
    fills,
    plan,
    density,
    spread,
    held,
    wire,
    inbox,
    cross,
    whole,
    guests,
    coefs,
    outbox,
    results,
    near_norm,
    far_norm,
    held_sem,
    end_send,
    end_recv,
    mid_send,
    mid_recv,
    final_send,
    final_recv,
    over_send,
    over_recv,
    guest_send,
    guest_recv,
    pass_send,
    pass_recv,
    coef_send,
    coef_recv,
    result_send,
    result_recv,
):
    c, z = lax.axis_index("cell"), lax.axis_index("gene")
    rows, comps = whole.shape
    half = rows // 2
    steps = half // PIECE
    share = guests.shape[1]
    own_steps = share // PIECE
    side = z // 2
    is_mid = (z + 1) // 2 % 2 == 1
    is_end = (z + 1) // 2 % 2 == 0
    mate = z + 1 - 2 * (z % 2)
    opposite = 3 - z
    near, far = side * half, half - side * half
    own_first = z % 2 * own_steps
    relations = (1, 2, 4, 6)

    def part(base, i):
        return pl.ds(pl.multiple_of(base + i * PIECE, PIECE), PIECE)

    def held_copy(base, i, k):
        at = part(base, i)
        return pltpu.make_async_copy(counts.at[at], held.at[at], held_sem.at[2 * i + k])

    def end_copy(base, i, k):
        at = part(base, i)
        return remote(wire.at[at], inbox.at[at], end_send.at[2 * i + k], end_recv.at[2 * i + k], gene=mate)

    def mid_copy(base, i):
        at = part(base, i)
        return remote(wire.at[at], cross.at[at], mid_send.at[i], mid_recv.at[i], gene=opposite)

    def final_copy(base, i, k):
        at = part(base, i)
        return remote(whole.at[at], whole.at[at], final_send.at[2 * i + k], final_recv.at[2 * i + k], gene=mate)

    def over_copy(base, i):
        at = part(base, i)
        return remote(whole.at[at], whole.at[at], over_send.at[i], over_recv.at[i], gene=opposite)

    def guest_copy(r, i, slot):
        j = i - own_first
        return remote(
            whole.at[part(near, i)],
            guests.at[slot, part(0, j)],
            guest_send.at[r * own_steps + j],
            guest_recv.at[r * own_steps + j],
            cell=flip(c, relations[r]),
        )

    def pass_copy(r, j, slot):
        at = part(0, j)
        return remote(
            guests.at[slot, at],
            guests.at[slot, at],
            pass_send.at[(r - 1) * own_steps + j],
            pass_recv.at[(r - 1) * own_steps + j],
            cell=flip(c, 1),
        )

    def coef_copy(mask, slot):
        return remote(
            coefs.at[slot], coefs.at[slot], coef_send.at[mask - 1], coef_recv.at[mask - 1], cell=flip(c, mask)
        )

    def result_copy(mask, slot):
        return remote(
            outbox, results.at[slot], result_send.at[mask - 1], result_recv.at[mask - 1], cell=flip(c, mask)
        )

    def offer(i):
        @pl.when((i >= own_first) & (i < own_first + own_steps))
        def _():
            for r in range(4):
                guest_copy(r, i, c).start()

    def product(base, i, k):
        held_copy(base, i, k).wait()
        return jnp.dot(held[part(base, i), :], loadings[...], preferred_element_type=jnp.float32)

    def loop(count, body):
        def step(i, carry):
            body(i)
            return carry

        lax.fori_loop(0, count, step, 0)

    @functools.partial(loop, steps)
    def _(i):
        held_copy(far, i, 0).start()
        held_copy(near, i, 1).start()

    barrier = pltpu.get_barrier_semaphore()
    for mask in range(1, cells):
        pl.semaphore_signal(barrier, inc=1, device_id={"cell": flip(c, mask)}, device_id_type=MESH)
    pl.semaphore_signal(barrier, inc=1, device_id={"gene": mate}, device_id_type=MESH)

    @pl.when(is_mid)
    def _():
        pl.semaphore_signal(barrier, inc=1, device_id={"gene": opposite}, device_id_type=MESH)

    picked = jnp.zeros(index.shape, jnp.float32)
    for entry in range(widths.shape[0]):
        picked = picked + jnp.where(index[...] == entry, widths[entry], 0.0)
    own_coef = 1.0 / (2.0 * comps * picked * picked)
    coefs[c] = jnp.broadcast_to(own_coef, (8, share))

    @pl.when(is_end)
    def _():
        pl.semaphore_wait(barrier, cells)

        @functools.partial(loop, steps)
        def _(i):
            for k, base in enumerate((far, near)):
                wire[part(base, i), :] = product(base, i, k).astype(wire.dtype)
                end_copy(base, i, k).start()

        for mask in range(1, cells):
            coef_copy(mask, c).start()

        @functools.partial(loop, steps)
        def _(i):
            final_copy(near, i, 1).wait_recv()
            offer(i)
            final_copy(far, i, 0).wait_recv()

        @functools.partial(loop, steps)
        def _(i):
            end_copy(far, i, 0).wait_send()
            end_copy(near, i, 1).wait_send()

    @pl.when(is_mid)
    def _():
        pl.semaphore_wait(barrier, cells + 1)
        for mask in range(1, cells):
            coef_copy(mask, c).start()

        @functools.partial(loop, steps)
        def _(i):
            far_part = product(far, i, 0)
            near_part = product(near, i, 1)
            end_copy(far, i, 0).wait_recv()
            far_part = far_part + inbox[part(far, i), :].astype(jnp.float32)
            wire[part(far, i), :] = far_part.astype(wire.dtype)
            mid_copy(far, i).start()

            @pl.when(i > 0)
            def _():
                over_copy(far, i - 1).wait_recv()
                final_copy(far, i - 1, 0).start()

            end_copy(near, i, 1).wait_recv()
            near_part = near_part + inbox[part(near, i), :].astype(jnp.float32)
            mid_copy(near, i).wait_recv()
            near_part = near_part + cross[part(near, i), :].astype(jnp.float32)
            whole[part(near, i), :] = near_part.astype(whole.dtype)
            over_copy(near, i).start()
            final_copy(near, i, 1).start()
            offer(i)

        over_copy(far, steps - 1).wait_recv()
        final_copy(far, steps - 1, 0).start()

        @functools.partial(loop, steps)
        def _(i):
            mid_copy(far, i).wait_send()
            over_copy(near, i).wait_send()
            final_copy(near, i, 1).wait_send()
            final_copy(far, i, 0).wait_send()

    @functools.partial(loop, own_steps)
    def _(j):
        for r in range(1, 4):
            slot = flip(c, relations[r])
            guest_copy(r, own_first + j, slot).wait_recv()
            pass_copy(r, j, slot).start()

    fill = fills[c]

    @functools.partial(loop, rows // TILE)
    def _(t):
        at = pl.ds(pl.multiple_of(t * TILE, TILE), TILE)
        keys = whole[at, :].astype(jnp.float32)
        norm = jnp.sum(keys * keys, axis=1, keepdims=True)
        live = t * TILE + lax.broadcasted_iota(jnp.int32, (TILE, 1), 0) < fill
        near_norm[at, :] = jnp.broadcast_to(jnp.where(live, norm, FAR), (TILE, 128))
        far_norm[at, :] = jnp.broadcast_to(jnp.where(live, norm, -FAR), (TILE, 128))

    def dot_t(a, b):
        return lax.dot_general(a, b, (((1,), (1,)), ((), ())), preferred_element_type=jnp.float32)

    def terms(queries, coef):
        square = queries.astype(jnp.float32)
        square = square * square
        high = square.astype(jnp.bfloat16)
        low = (square - high.astype(jnp.float32)).astype(jnp.bfloat16)
        ones = jnp.ones((8, comps), jnp.bfloat16)
        norm = dot_t(ones, high) + dot_t(ones, low)
        rate = coef * (-1.0 / math.log(2.0))
        doubled = queries * jnp.asarray(-2.0, queries.dtype)

        def step(t, carry):
            total, top = carry
            at = pl.ds(pl.multiple_of(t * TILE, TILE), TILE)
            inner = dot_t(whole[at, :], doubled).reshape(TILE // 8, 8, share)
            closest = jnp.concatenate([near_norm[at, :].reshape(TILE // 8, 8, 128)] * (share // 128), axis=2)
            farthest = jnp.concatenate([far_norm[at, :].reshape(TILE // 8, 8, 128)] * (share // 128), axis=2)
            base = inner + norm[None]
            weight = jnp.exp2(jnp.maximum(base + closest, 0.0) * rate[None])
            total = total + jnp.sum(weight, axis=0)
            top = jnp.maximum(top, jnp.max(base + farthest, axis=0))
            return total, top

        zero = jnp.zeros((8, share), jnp.float32)
        total, top = lax.fori_loop(0, rows // TILE, step, (zero, zero))
        return jnp.sum(total, axis=0, keepdims=True), jnp.max(top, axis=0, keepdims=True)

    own_rows = pl.ds(pl.multiple_of(z * share, share), share)
    total, top = terms(whole[own_rows, :], coefs[c])

    @functools.partial(loop, own_steps)
    def _(j):
        guest_copy(0, own_first + j, flip(c, 1)).wait_recv()
        for r in range(1, 4):
            pass_copy(r, j, flip(c, relations[r] + 1)).wait_recv()

    for mask in range(1, cells):
        coef_copy(mask, flip(c, mask)).wait_recv()

    opposite_cell = flip(c, cells - 1)
    other_cell = jnp.bitwise_and(jnp.bitwise_xor(c, plan[0] + plan[1] - (cells - 1)), cells - 1)
    for at, guest in ((0, opposite_cell), (2, other_cell)):
        more, most = terms(guests[guest], coefs[guest])
        outbox[at : at + 1, :] = more
        outbox[at + 1 : at + 2, :] = most
    outbox[4:8, :] = jnp.zeros((4, share), jnp.float32)
    for mask in range(1, cells):
        result_copy(mask, c).start()

    @functools.partial(loop, own_steps)
    def _(j):
        for r in range(4):
            guest_copy(r, own_first + j, c).wait_send()
        for r in range(1, 4):
            pass_copy(r, j, flip(c, relations[r])).wait_send()

    for mask in range(1, cells):
        coef_copy(mask, c).wait_send()
    for mask in range(1, cells):
        result_copy(mask, flip(c, mask)).wait_recv()
    first, second = results[opposite_cell], results[other_cell]
    total = total + first[0:1] + second[2:3]
    top = jnp.maximum(jnp.maximum(top, first[1:2]), second[3:4])
    qlive = z * share + lax.broadcasted_iota(jnp.int32, (1, share), 1) < fill
    density[...] = jnp.where(qlive, jnp.log(total), 0.0)
    spread[...] = jnp.where(qlive, jnp.sqrt(top / comps), 0.0)
    for mask in range(1, cells):
        result_copy(mask, c).wait_send()


def by_kernel(counts, loadings, kernel_widths, width_index, block_fill, plan):
    cells, groups = lax.axis_size("cell"), lax.axis_size("gene")
    rows, comps = counts.shape[0], loadings.shape[1]
    share = rows // groups
    steps, own_steps = rows // 2 // PIECE, share // PIECE
    block = pltpu.VMEM((rows, comps), jnp.bfloat16)
    dma = pltpu.SemaphoreType.DMA
    vmem, smem = pl.BlockSpec(memory_space=pltpu.VMEM), pl.BlockSpec(memory_space=pltpu.SMEM)
    out = jax.ShapeDtypeStruct((1, share), jnp.float32)
    density, spread = pl.pallas_call(
        functools.partial(kernel, cells),
        out_shape=(out, out),
        in_specs=[pl.BlockSpec(memory_space=pl.ANY), vmem, vmem, smem, smem, smem],
        out_specs=(vmem, vmem),
        scratch_shapes=[
            pltpu.VMEM(counts.shape, counts.dtype),
            block,
            block,
            block,
            block,
            pltpu.VMEM((cells, share, comps), jnp.bfloat16),
            pltpu.VMEM((cells, 8, share), jnp.float32),
            pltpu.VMEM((8, share), jnp.float32),
            pltpu.VMEM((cells, 8, share), jnp.float32),
            pltpu.VMEM((rows, 128), jnp.float32),
            pltpu.VMEM((rows, 128), jnp.float32),
            dma((2 * steps,)),
            dma((2 * steps,)),
            dma((2 * steps,)),
            dma((steps,)),
            dma((steps,)),
            dma((2 * steps,)),
            dma((2 * steps,)),
            dma((steps,)),
            dma((steps,)),
            dma((4 * own_steps,)),
            dma((4 * own_steps,)),
            dma((3 * own_steps,)),
            dma((3 * own_steps,)),
            dma((cells - 1,)),
            dma((cells - 1,)),
            dma((cells - 1,)),
            dma((cells - 1,)),
        ],
        compiler_params=pltpu.CompilerParams(
            collective_id=0, has_side_effects=True, vmem_limit_bytes=48 * 1024 * 1024
        ),
    )(counts, loadings, width_index.reshape(1, share), kernel_widths, block_fill, plan)
    return density.reshape(share), spread.reshape(share)


def exchange(value, stride, axis):
    cells = lax.axis_size(axis)
    for bit in range(cells.bit_length() - 1):
        pairs = [(source, source ^ (1 << bit)) for source in range(cells)]
        chosen = jnp.bitwise_and(jnp.right_shift(stride, bit), 1) == 1
        value = lax.cond(
            chosen,
            lambda v: jax.tree.map(lambda a: lax.ppermute(a, axis, pairs), v),
            lambda v: v,
            value,
        )
    return value


def block_terms(queries, coef, keys, fill):
    qf = queries.astype(jnp.float32)
    kf = keys.astype(jnp.float32)
    qnorm = jnp.sum(qf * qf, axis=1)
    knorm = jnp.sum(kf * kf, axis=1)
    inner = jnp.einsum("qc,kc->qk", queries, keys, preferred_element_type=jnp.float32)
    dist = jnp.maximum(qnorm[:, None] + knorm[None, :] - 2.0 * inner, 0.0)
    live = jnp.arange(keys.shape[0], dtype=jnp.int32)[None, :] < fill
    kernel = jnp.where(live, jnp.exp(-dist * coef[:, None]), 0.0)
    return (jnp.sum(kernel, axis=1), jnp.max(jnp.where(live, dist, 0.0), axis=1))


def lookup(table, index):
    slots = jnp.arange(table.shape[0], dtype=jnp.int32)
    return jnp.sum(jnp.where(slots == index, table, 0))


def by_exchange(counts, loadings, kernel_widths, width_index, block_fill, plan):
    groups = lax.axis_size("gene")
    share = counts.shape[0] // groups
    gene_pos = lax.axis_index("gene")
    own_fill = lookup(block_fill, lax.axis_index("cell"))
    partial_scores = jnp.dot(counts, loadings, preferred_element_type=jnp.float32)
    mine = lax.psum_scatter(partial_scores, "gene", scatter_dimension=0, tiled=True)
    mine = mine.astype(jnp.bfloat16)
    whole = lax.all_gather(mine, "gene", axis=0, tiled=True)
    comps = whole.shape[1]
    picked = width_index[:, None] == jnp.arange(kernel_widths.shape[0], dtype=jnp.int32)[None, :]
    width = jnp.sum(jnp.where(picked, kernel_widths[None, :], 0.0), axis=1)
    coef = 1.0 / (2.0 * comps * width * width)
    total, top = block_terms(mine, coef, whole, own_fill)
    for step in range(plan.shape[0]):
        guests, guest_coef = exchange((mine, coef), plan[step], "cell")
        terms = block_terms(guests, guest_coef, whole, own_fill)
        more, far = exchange(terms, plan[step], "cell")
        total = total + more
        top = jnp.maximum(top, far)
    positions = gene_pos * share + jnp.arange(share, dtype=jnp.int32)
    qlive = positions < own_fill
    density = jnp.where(qlive, jnp.log(total), 0.0)
    spread = jnp.where(qlive, jnp.sqrt(top / comps), 0.0)
    return (density, spread)


def solution(mesh):
    placed = (P("cell", "gene"), P("gene", None), P(), P(("cell", "gene")), P(), P())
    small = mesh.shape["cell"] == 8 and mesh.shape["gene"] == 4
    return jax.shard_map(
        by_kernel if small else by_exchange,
        mesh=mesh,
        in_specs=placed,
        out_specs=(P(("cell", "gene")), P(("cell", "gene"))),
        check_vma=False,
    )
```

```python
import functools
import math
import jax
import jax.numpy as jnp
from jax import lax
from jax.experimental import pallas as pl
from jax.experimental.pallas import tpu as pltpu
from jax.sharding import PartitionSpec as P

MESH = pl.DeviceIdType.MESH
PIECE = 128
TILE = 256
FAR = 1e30


def flip(place, mask):
    for bit in range(mask.bit_length()):
        if (mask >> bit) & 1:
            place = place + (1 << bit) * (1 - 2 * (place // (1 << bit) % 2))
    return place


def remote(src, dst, send, recv, **device):
    return pltpu.make_async_remote_copy(
        src_ref=src, dst_ref=dst, send_sem=send, recv_sem=recv, device_id=device, device_id_type=MESH
    )


def kernel(
    cells,
    counts,
    loadings_in,
    index_in,
    widths_in,
    fills_in,
    plan_in,
    density,
    spread,
    loadings,
    index,
    widths,
    fills,
    plan,
    small_sem,
    held,
    wire,
    inbox,
    cross,
    whole,
    guests,
    coefs,
    outbox,
    results,
    near_norm,
    far_norm,
    held_sem,
    end_send,
    end_recv,
    mid_send,
    mid_recv,
    final_send,
    final_recv,
    over_send,
    over_recv,
    guest_send,
    guest_recv,
    pass_send,
    pass_recv,
    coef_send,
    coef_recv,
    result_send,
    result_recv,
):
    c, z = lax.axis_index("cell"), lax.axis_index("gene")
    rows, comps = whole.shape
    half = rows // 2
    steps = half // PIECE
    share = guests.shape[1]
    own_steps = share // PIECE
    side = z // 2
    is_mid = (z + 1) // 2 % 2 == 1
    is_end = (z + 1) // 2 % 2 == 0
    mate = z + 1 - 2 * (z % 2)
    opposite = 3 - z
    near, far = side * half, half - side * half
    relations = (1, 2, 4, 6)

    def part(base, i):
        return piece(base, i % 2 * own_steps + i // 2)

    def piece(base, i):
        return pl.ds(pl.multiple_of(base + i * PIECE, PIECE), PIECE)

    def held_copy(base, i, k):
        at = part(base, i)
        return pltpu.make_async_copy(counts.at[at], held.at[at], held_sem.at[2 * i + k])

    def end_copy(base, i, k):
        at = part(base, i)
        return remote(wire.at[at], inbox.at[at], end_send.at[2 * i + k], end_recv.at[2 * i + k], gene=mate)

    def mid_copy(base, i):
        at = part(base, i)
        return remote(wire.at[at], cross.at[at], mid_send.at[i], mid_recv.at[i], gene=opposite)

    def final_copy(base, i, k):
        at = part(base, i)
        return remote(whole.at[at], whole.at[at], final_send.at[2 * i + k], final_recv.at[2 * i + k], gene=mate)

    def over_copy(base, i):
        at = part(base, i)
        return remote(whole.at[at], whole.at[at], over_send.at[i], over_recv.at[i], gene=opposite)

    def guest_copy(r, i, slot):
        j = i // 2
        return remote(
            whole.at[part(near, i)],
            guests.at[slot, piece(0, j)],
            guest_send.at[r * own_steps + j],
            guest_recv.at[r * own_steps + j],
            cell=flip(c, relations[r]),
        )

    def pass_copy(r, j, slot):
        at = piece(0, j)
        return remote(
            guests.at[slot, at],
            guests.at[slot, at],
            pass_send.at[(r - 1) * own_steps + j],
            pass_recv.at[(r - 1) * own_steps + j],
            cell=flip(c, 1),
        )

    def coef_copy(mask, slot):
        return remote(
            coefs.at[slot], coefs.at[slot], coef_send.at[mask - 1], coef_recv.at[mask - 1], cell=flip(c, mask)
        )

    def result_copy(mask, slot):
        return remote(
            outbox, results.at[slot], result_send.at[mask - 1], result_recv.at[mask - 1], cell=flip(c, mask)
        )

    def offer(i):
        @pl.when(i % 2 == z % 2)
        def _():
            for r in range(4):
                guest_copy(r, i, c).start()

    def product(base, i, k):
        held_copy(base, i, k).wait()
        return jnp.dot(held[part(base, i), :], loadings[...], preferred_element_type=jnp.float32)

    def norms(base, i):
        at = part(base, i)
        keys = whole[at, :].astype(jnp.float32)
        norm = jnp.sum(keys * keys, axis=1, keepdims=True)
        first = base + (i % 2 * own_steps + i // 2) * PIECE
        live = first + lax.broadcasted_iota(jnp.int32, (PIECE, 1), 0) < fill
        near_norm[at, :] = jnp.broadcast_to(jnp.where(live, norm, FAR), (PIECE, 128))
        far_norm[at, :] = jnp.broadcast_to(jnp.where(live, norm, -FAR), (PIECE, 128))

    def loop(count, body):
        def step(i, carry):
            body(i)
            return carry

        lax.fori_loop(0, count, step, 0)

    small = [
        pltpu.make_async_copy(source, target, small_sem.at[k])
        for k, (source, target) in enumerate(
            (
                (loadings_in, loadings),
                (index_in, index),
                (widths_in, widths),
                (fills_in, fills),
                (plan_in, plan),
            )
        )
    ]
    small[0].start()
    held_copy(far, 0, 0).start()
    held_copy(near, 0, 1).start()
    for copy in small[1:]:
        copy.start()

    @functools.partial(loop, steps - 1)
    def _(i):
        held_copy(far, i + 1, 0).start()
        held_copy(near, i + 1, 1).start()

    barrier = pltpu.get_barrier_semaphore()
    for mask in range(1, cells):
        pl.semaphore_signal(barrier, inc=1, device_id={"cell": flip(c, mask)}, device_id_type=MESH)
    pl.semaphore_signal(barrier, inc=1, device_id={"gene": mate}, device_id_type=MESH)

    @pl.when(is_mid)
    def _():
        pl.semaphore_signal(barrier, inc=1, device_id={"gene": opposite}, device_id_type=MESH)

    for copy in small:
        copy.wait()
    fill = fills[c]
    picked = jnp.zeros(index.shape, jnp.float32)
    for entry in range(widths.shape[0]):
        picked = picked + jnp.where(index[...] == entry, widths[entry], 0.0)
    own_coef = 1.0 / (2.0 * comps * picked * picked)
    coefs[c] = jnp.broadcast_to(own_coef, (8, share))

    @pl.when(is_end)
    def _():
        pl.semaphore_wait(barrier, cells)

        @functools.partial(loop, steps)
        def _(i):
            for k, base in enumerate((far, near)):
                wire[part(base, i), :] = product(base, i, k).astype(wire.dtype)
                end_copy(base, i, k).start()

        for mask in range(1, cells):
            coef_copy(mask, c).start()

        @functools.partial(loop, steps)
        def _(i):
            final_copy(near, i, 1).wait_recv()
            offer(i)
            norms(near, i)
            final_copy(far, i, 0).wait_recv()
            norms(far, i)

        @functools.partial(loop, steps)
        def _(i):
            end_copy(far, i, 0).wait_send()
            end_copy(near, i, 1).wait_send()

    @pl.when(is_mid)
    def _():
        pl.semaphore_wait(barrier, cells + 1)
        for mask in range(1, cells):
            coef_copy(mask, c).start()

        @functools.partial(loop, steps + 2)
        def _(i):
            @pl.when(i < steps)
            def _():
                total = product(far, i, 0)
                end_copy(far, i, 0).wait_recv()
                total = total + inbox[part(far, i), :].astype(jnp.float32)
                wire[part(far, i), :] = total.astype(wire.dtype)
                mid_copy(far, i).start()

            @pl.when(i >= 2)
            def _():
                over_copy(far, i - 2).wait_recv()
                final_copy(far, i - 2, 0).start()
                norms(far, i - 2)

            @pl.when((i >= 1) & (i <= steps))
            def _():
                total = product(near, i - 1, 1)
                end_copy(near, i - 1, 1).wait_recv()
                total = total + inbox[part(near, i - 1), :].astype(jnp.float32)
                mid_copy(near, i - 1).wait_recv()
                total = total + cross[part(near, i - 1), :].astype(jnp.float32)
                whole[part(near, i - 1), :] = total.astype(whole.dtype)
                over_copy(near, i - 1).start()
                final_copy(near, i - 1, 1).start()
                offer(i - 1)
                norms(near, i - 1)

        @functools.partial(loop, steps)
        def _(i):
            mid_copy(far, i).wait_send()
            over_copy(near, i).wait_send()
            final_copy(near, i, 1).wait_send()
            final_copy(far, i, 0).wait_send()

    @functools.partial(loop, own_steps)
    def _(j):
        for r in range(1, 4):
            slot = flip(c, relations[r])
            guest_copy(r, 2 * j + z % 2, slot).wait_recv()
            pass_copy(r, j, slot).start()

    def dot_t(a, b):
        return lax.dot_general(a, b, (((1,), (1,)), ((), ())), preferred_element_type=jnp.float32)

    def terms(queries, coef):
        square = queries.astype(jnp.float32)
        square = square * square
        high = square.astype(jnp.bfloat16)
        low = (square - high.astype(jnp.float32)).astype(jnp.bfloat16)
        ones = jnp.ones((8, comps), jnp.bfloat16)
        norm = dot_t(ones, high) + dot_t(ones, low)
        rate = coef * (-1.0 / math.log(2.0))
        doubled = queries * jnp.asarray(-2.0, queries.dtype)

        def step(t, carry):
            total, top = carry
            at = pl.ds(pl.multiple_of(t * TILE, TILE), TILE)
            inner = dot_t(whole[at, :], doubled).reshape(TILE // 8, 8, share)
            closest = jnp.concatenate([near_norm[at, :].reshape(TILE // 8, 8, 128)] * (share // 128), axis=2)
            farthest = jnp.concatenate([far_norm[at, :].reshape(TILE // 8, 8, 128)] * (share // 128), axis=2)
            base = inner + norm[None]
            weight = jnp.exp2(jnp.maximum(base + closest, 0.0) * rate[None])
            total = total + jnp.sum(weight, axis=0)
            top = jnp.maximum(top, jnp.max(base + farthest, axis=0))
            return total, top

        zero = jnp.zeros((8, share), jnp.float32)
        total, top = lax.fori_loop(0, rows // TILE, step, (zero, zero))
        return jnp.sum(total, axis=0, keepdims=True), jnp.max(top, axis=0, keepdims=True)

    own_rows = pl.ds(pl.multiple_of(z * share, share), share)
    total, top = terms(whole[own_rows, :], coefs[c])

    @functools.partial(loop, own_steps)
    def _(j):
        guest_copy(0, 2 * j + z % 2, flip(c, 1)).wait_recv()
        for r in range(1, 4):
            pass_copy(r, j, flip(c, relations[r] + 1)).wait_recv()

    for mask in range(1, cells):
        coef_copy(mask, flip(c, mask)).wait_recv()

    opposite_cell = flip(c, cells - 1)
    other_cell = jnp.bitwise_and(jnp.bitwise_xor(c, plan[0] + plan[1] - (cells - 1)), cells - 1)
    for at, guest in ((0, opposite_cell), (2, other_cell)):
        more, most = terms(guests[guest], coefs[guest])
        outbox[at : at + 1, :] = more
        outbox[at + 1 : at + 2, :] = most
    outbox[4:8, :] = jnp.zeros((4, share), jnp.float32)
    for mask in range(1, cells):
        result_copy(mask, c).start()

    @functools.partial(loop, own_steps)
    def _(j):
        for r in range(4):
            guest_copy(r, 2 * j + z % 2, c).wait_send()
        for r in range(1, 4):
            pass_copy(r, j, flip(c, relations[r])).wait_send()

    for mask in range(1, cells):
        coef_copy(mask, c).wait_send()
    for mask in range(1, cells):
        result_copy(mask, flip(c, mask)).wait_recv()
    first, second = results[opposite_cell], results[other_cell]
    total = total + first[0:1] + second[2:3]
    top = jnp.maximum(jnp.maximum(top, first[1:2]), second[3:4])
    qlive = z * share + lax.broadcasted_iota(jnp.int32, (1, share), 1) < fill
    density[...] = jnp.where(qlive, jnp.log(total), 0.0)
    spread[...] = jnp.where(qlive, jnp.sqrt(top / comps), 0.0)
    for mask in range(1, cells):
        result_copy(mask, c).wait_send()


def by_kernel(counts, loadings, kernel_widths, width_index, block_fill, plan):
    cells, groups = lax.axis_size("cell"), lax.axis_size("gene")
    rows, comps = counts.shape[0], loadings.shape[1]
    share = rows // groups
    steps, own_steps = rows // 2 // PIECE, share // PIECE
    block = pltpu.VMEM((rows, comps), jnp.bfloat16)
    dma = pltpu.SemaphoreType.DMA
    vmem = pl.BlockSpec(memory_space=pltpu.VMEM)
    out = jax.ShapeDtypeStruct((1, share), jnp.float32)
    density, spread = pl.pallas_call(
        functools.partial(kernel, cells),
        out_shape=(out, out),
        in_specs=[pl.BlockSpec(memory_space=pltpu.HBM)] * 6,
        out_specs=(vmem, vmem),
        scratch_shapes=[
            pltpu.VMEM(loadings.shape, loadings.dtype),
            pltpu.VMEM((1, share), width_index.dtype),
            pltpu.SMEM(kernel_widths.shape, kernel_widths.dtype),
            pltpu.SMEM(block_fill.shape, block_fill.dtype),
            pltpu.SMEM(plan.shape, plan.dtype),
            dma((5,)),
            pltpu.VMEM(counts.shape, counts.dtype),
            block,
            block,
            block,
            block,
            pltpu.VMEM((cells, share, comps), jnp.bfloat16),
            pltpu.VMEM((cells, 8, share), jnp.float32),
            pltpu.VMEM((8, share), jnp.float32),
            pltpu.VMEM((cells, 8, share), jnp.float32),
            pltpu.VMEM((rows, 128), jnp.float32),
            pltpu.VMEM((rows, 128), jnp.float32),
            dma((2 * steps,)),
            dma((2 * steps,)),
            dma((2 * steps,)),
            dma((steps,)),
            dma((steps,)),
            dma((2 * steps,)),
            dma((2 * steps,)),
            dma((steps,)),
            dma((steps,)),
            dma((4 * own_steps,)),
            dma((4 * own_steps,)),
            dma((3 * own_steps,)),
            dma((3 * own_steps,)),
            dma((cells - 1,)),
            dma((cells - 1,)),
            dma((cells - 1,)),
            dma((cells - 1,)),
        ],
        compiler_params=pltpu.CompilerParams(
            collective_id=0, has_side_effects=True, vmem_limit_bytes=63 * 1024 * 1024
        ),
    )(counts, loadings, width_index.reshape(1, share), kernel_widths, block_fill, plan)
    return density.reshape(share), spread.reshape(share)


def exchange(value, stride, axis):
    cells = lax.axis_size(axis)
    for bit in range(cells.bit_length() - 1):
        pairs = [(source, source ^ (1 << bit)) for source in range(cells)]
        chosen = jnp.bitwise_and(jnp.right_shift(stride, bit), 1) == 1
        value = lax.cond(
            chosen,
            lambda v: jax.tree.map(lambda a: lax.ppermute(a, axis, pairs), v),
            lambda v: v,
            value,
        )
    return value


def block_terms(queries, coef, keys, fill):
    qf = queries.astype(jnp.float32)
    kf = keys.astype(jnp.float32)
    qnorm = jnp.sum(qf * qf, axis=1)
    knorm = jnp.sum(kf * kf, axis=1)
    inner = jnp.einsum("qc,kc->qk", queries, keys, preferred_element_type=jnp.float32)
    dist = jnp.maximum(qnorm[:, None] + knorm[None, :] - 2.0 * inner, 0.0)
    live = jnp.arange(keys.shape[0], dtype=jnp.int32)[None, :] < fill
    kernel = jnp.where(live, jnp.exp(-dist * coef[:, None]), 0.0)
    return (jnp.sum(kernel, axis=1), jnp.max(jnp.where(live, dist, 0.0), axis=1))


def lookup(table, index):
    slots = jnp.arange(table.shape[0], dtype=jnp.int32)
    return jnp.sum(jnp.where(slots == index, table, 0))


def by_exchange(counts, loadings, kernel_widths, width_index, block_fill, plan):
    groups = lax.axis_size("gene")
    share = counts.shape[0] // groups
    gene_pos = lax.axis_index("gene")
    own_fill = lookup(block_fill, lax.axis_index("cell"))
    partial_scores = jnp.dot(counts, loadings, preferred_element_type=jnp.float32)
    mine = lax.psum_scatter(partial_scores, "gene", scatter_dimension=0, tiled=True)
    mine = mine.astype(jnp.bfloat16)
    whole = lax.all_gather(mine, "gene", axis=0, tiled=True)
    comps = whole.shape[1]
    picked = width_index[:, None] == jnp.arange(kernel_widths.shape[0], dtype=jnp.int32)[None, :]
    width = jnp.sum(jnp.where(picked, kernel_widths[None, :], 0.0), axis=1)
    coef = 1.0 / (2.0 * comps * width * width)
    total, top = block_terms(mine, coef, whole, own_fill)
    for step in range(plan.shape[0]):
        guests, guest_coef = exchange((mine, coef), plan[step], "cell")
        terms = block_terms(guests, guest_coef, whole, own_fill)
        more, far = exchange(terms, plan[step], "cell")
        total = total + more
        top = jnp.maximum(top, far)
    positions = gene_pos * share + jnp.arange(share, dtype=jnp.int32)
    qlive = positions < own_fill
    density = jnp.where(qlive, jnp.log(total), 0.0)
    spread = jnp.where(qlive, jnp.sqrt(top / comps), 0.0)
    return (density, spread)


def solution(mesh):
    placed = (P("cell", "gene"), P("gene", None), P(), P(("cell", "gene")), P(), P())
    small = mesh.shape["cell"] == 8 and mesh.shape["gene"] == 4
    return jax.shard_map(
        by_kernel if small else by_exchange,
        mesh=mesh,
        in_specs=placed,
        out_specs=(P(("cell", "gene")), P(("cell", "gene"))),
        check_vma=False,
    )
```

```python
import functools
import math
import jax
import jax.numpy as jnp
from jax import lax
from jax.experimental import pallas as pl
from jax.experimental.pallas import tpu as pltpu
from jax.sharding import PartitionSpec as P

MESH = pl.DeviceIdType.MESH
PIECE = 128
TILE = 256
FAR = 1e30


def flip(place, mask):
    for bit in range(mask.bit_length()):
        if (mask >> bit) & 1:
            place = place + (1 << bit) * (1 - 2 * (place // (1 << bit) % 2))
    return place


def remote(src, dst, send, recv, **device):
    return pltpu.make_async_remote_copy(
        src_ref=src, dst_ref=dst, send_sem=send, recv_sem=recv, device_id=device, device_id_type=MESH
    )


def kernel(
    cells,
    counts,
    loadings_in,
    index_in,
    widths_in,
    fills_in,
    plan_in,
    density,
    spread,
    loadings,
    index,
    widths,
    fills,
    plan,
    small_sem,
    held,
    wire,
    inbox,
    cross,
    whole,
    guests,
    coefs,
    outbox,
    results,
    near_norm,
    far_norm,
    turned_queries,
    even,
    odd,
    held_sem,
    end_send,
    end_recv,
    mid_send,
    mid_recv,
    final_send,
    final_recv,
    over_send,
    over_recv,
    guest_send,
    guest_recv,
    pass_send,
    pass_recv,
    coef_send,
    coef_recv,
    result_send,
    result_recv,
):
    c, z = lax.axis_index("cell"), lax.axis_index("gene")
    rows, comps = whole.shape
    half = rows // 2
    steps = half // PIECE
    share = guests.shape[1]
    own_steps = share // PIECE
    side = z // 2
    is_mid = (z + 1) // 2 % 2 == 1
    is_end = (z + 1) // 2 % 2 == 0
    mate = z + 1 - 2 * (z % 2)
    opposite = 3 - z
    near, far = side * half, half - side * half
    relations = (1, 2, 4, 6)

    def part(base, i):
        return piece(base, i % 2 * own_steps + i // 2)

    def piece(base, i):
        return pl.ds(pl.multiple_of(base + i * PIECE, PIECE), PIECE)

    def held_copy(base, i, k):
        at = part(base, i)
        return pltpu.make_async_copy(counts.at[at], held.at[at], held_sem.at[2 * i + k])

    def end_copy(base, i, k):
        at = part(base, i)
        return remote(wire.at[at], inbox.at[at], end_send.at[2 * i + k], end_recv.at[2 * i + k], gene=mate)

    def mid_copy(base, i):
        at = part(base, i)
        return remote(wire.at[at], cross.at[at], mid_send.at[i], mid_recv.at[i], gene=opposite)

    def final_copy(base, i, k):
        at = part(base, i)
        return remote(whole.at[at], whole.at[at], final_send.at[2 * i + k], final_recv.at[2 * i + k], gene=mate)

    def over_copy(base, i):
        at = part(base, i)
        return remote(whole.at[at], whole.at[at], over_send.at[i], over_recv.at[i], gene=opposite)

    def guest_copy(r, i, slot):
        j = i // 2
        return remote(
            whole.at[part(near, i)],
            guests.at[slot, piece(0, j)],
            guest_send.at[r * own_steps + j],
            guest_recv.at[r * own_steps + j],
            cell=flip(c, relations[r]),
        )

    def pass_copy(r, j, slot):
        at = piece(0, j)
        return remote(
            guests.at[slot, at],
            guests.at[slot, at],
            pass_send.at[(r - 1) * own_steps + j],
            pass_recv.at[(r - 1) * own_steps + j],
            cell=flip(c, 1),
        )

    def coef_copy(mask, slot):
        return remote(
            coefs.at[slot], coefs.at[slot], coef_send.at[mask - 1], coef_recv.at[mask - 1], cell=flip(c, mask)
        )

    def result_copy(mask, slot):
        return remote(
            outbox, results.at[slot], result_send.at[mask - 1], result_recv.at[mask - 1], cell=flip(c, mask)
        )

    def offer(i):
        @pl.when(i % 2 == z % 2)
        def _():
            for r in range(4):
                guest_copy(r, i, c).start()

    def product(base, i, k):
        held_copy(base, i, k).wait()
        return jnp.dot(held[part(base, i), :], loadings[...], preferred_element_type=jnp.float32)

    def norms(base, i):
        at = part(base, i)
        keys = whole[at, :].astype(jnp.float32)
        norm = jnp.sum(keys * keys, axis=1, keepdims=True)
        first = base + (i % 2 * own_steps + i // 2) * PIECE
        live = first + lax.broadcasted_iota(jnp.int32, (PIECE, 1), 0) < fill
        near_norm[at, :] = jnp.broadcast_to(jnp.where(live, norm, FAR), (PIECE, 128))
        far_norm[at, :] = jnp.broadcast_to(jnp.where(live, norm, -FAR), (PIECE, 128))

    def loop(count, body):
        def step(i, carry):
            body(i)
            return carry

        lax.fori_loop(0, count, step, 0)

    small = [
        pltpu.make_async_copy(source, target, small_sem.at[k])
        for k, (source, target) in enumerate(
            (
                (loadings_in, loadings),
                (index_in, index),
                (widths_in, widths),
                (fills_in, fills),
                (plan_in, plan),
            )
        )
    ]
    small[0].start()
    held_copy(far, 0, 0).start()
    held_copy(near, 0, 1).start()
    for copy in small[1:]:
        copy.start()

    @functools.partial(loop, steps - 1)
    def _(i):
        held_copy(far, i + 1, 0).start()
        held_copy(near, i + 1, 1).start()

    barrier = pltpu.get_barrier_semaphore()
    for mask in range(1, cells):
        pl.semaphore_signal(barrier, inc=1, device_id={"cell": flip(c, mask)}, device_id_type=MESH)
    pl.semaphore_signal(barrier, inc=1, device_id={"gene": mate}, device_id_type=MESH)

    @pl.when(is_mid)
    def _():
        pl.semaphore_signal(barrier, inc=1, device_id={"gene": opposite}, device_id_type=MESH)

    for copy in small:
        copy.wait()
    fill = fills[c]
    picked = jnp.zeros(index.shape, jnp.float32)
    for entry in range(widths.shape[0]):
        picked = picked + jnp.where(index[...] == entry, widths[entry], 0.0)
    own_coef = 1.0 / (2.0 * comps * picked * picked)
    coefs[c] = jnp.broadcast_to(own_coef, (8, share))

    @pl.when(is_end)
    def _():
        pl.semaphore_wait(barrier, cells)

        @functools.partial(loop, steps)
        def _(i):
            for k, base in enumerate((far, near)):
                wire[part(base, i), :] = product(base, i, k).astype(wire.dtype)
                end_copy(base, i, k).start()

        for mask in range(1, cells):
            coef_copy(mask, c).start()

        @functools.partial(loop, steps)
        def _(i):
            final_copy(near, i, 1).wait_recv()
            offer(i)
            norms(near, i)
            final_copy(far, i, 0).wait_recv()
            norms(far, i)

        @functools.partial(loop, steps)
        def _(i):
            end_copy(far, i, 0).wait_send()
            end_copy(near, i, 1).wait_send()

    @pl.when(is_mid)
    def _():
        pl.semaphore_wait(barrier, cells + 1)
        for mask in range(1, cells):
            coef_copy(mask, c).start()

        @functools.partial(loop, steps + 2)
        def _(i):
            @pl.when(i < steps)
            def _():
                total = product(far, i, 0)
                end_copy(far, i, 0).wait_recv()
                total = total + inbox[part(far, i), :].astype(jnp.float32)
                wire[part(far, i), :] = total.astype(wire.dtype)
                mid_copy(far, i).start()

            @pl.when(i >= 2)
            def _():
                over_copy(far, i - 2).wait_recv()
                final_copy(far, i - 2, 0).start()
                norms(far, i - 2)

            @pl.when((i >= 1) & (i <= steps))
            def _():
                total = product(near, i - 1, 1)
                end_copy(near, i - 1, 1).wait_recv()
                total = total + inbox[part(near, i - 1), :].astype(jnp.float32)
                mid_copy(near, i - 1).wait_recv()
                total = total + cross[part(near, i - 1), :].astype(jnp.float32)
                whole[part(near, i - 1), :] = total.astype(whole.dtype)
                over_copy(near, i - 1).start()
                final_copy(near, i - 1, 1).start()
                offer(i - 1)
                norms(near, i - 1)

        @functools.partial(loop, steps)
        def _(i):
            mid_copy(far, i).wait_send()
            over_copy(near, i).wait_send()
            final_copy(near, i, 1).wait_send()
            final_copy(far, i, 0).wait_send()

    def forward(j):
        for r in range(1, 4):
            slot = flip(c, relations[r])
            guest_copy(r, 2 * j + z % 2, slot).wait_recv()
            pass_copy(r, j, slot).start()

    loop(own_steps - 1, forward)

    def terms(queries, coef):
        turned = queries.astype(jnp.float32).T
        norm = jnp.broadcast_to(jnp.sum(turned * turned, axis=0, keepdims=True), (8, share))
        turned_queries[...] = (turned * -2.0).astype(turned_queries.dtype)
        rate = coef * (-1.0 / math.log(2.0))
        tiles = rows // TILE

        def multiply(t, target):
            at = pl.ds(pl.multiple_of(t * TILE, TILE), TILE)
            target[...] = jnp.dot(whole[at, :], turned_queries[...], preferred_element_type=jnp.float32)

        def collect(t, source, total, top):
            for group in range(TILE // 8):
                at = pl.ds(pl.multiple_of(t * TILE + group * 8, 8), 8)
                base = source[group * 8 : group * 8 + 8, :] + norm
                closest = jnp.concatenate([near_norm[at, :]] * (share // 128), axis=1)
                farthest = jnp.concatenate([far_norm[at, :]] * (share // 128), axis=1)
                total = total + jnp.exp2(jnp.maximum(base + closest, 0.0) * rate)
                top = jnp.maximum(top, base + farthest)
            return total, top

        def step(t, carry):
            total, top = carry
            multiply(2 * t + 1, odd)
            total, top = collect(2 * t, even, total, top)
            multiply(jnp.minimum(2 * t + 2, tiles - 1), even)
            return collect(2 * t + 1, odd, total, top)

        zero = jnp.zeros((8, share), jnp.float32)
        multiply(0, even)
        total, top = lax.fori_loop(0, tiles // 2, step, (zero, zero))
        return jnp.sum(total, axis=0, keepdims=True), jnp.max(top, axis=0, keepdims=True)

    own_rows = pl.ds(pl.multiple_of(z * share, share), share)
    total, top = terms(whole[own_rows, :], coefs[c])
    forward(own_steps - 1)

    @functools.partial(loop, own_steps)
    def _(j):
        guest_copy(0, 2 * j + z % 2, flip(c, 1)).wait_recv()
        for r in range(1, 4):
            pass_copy(r, j, flip(c, relations[r] + 1)).wait_recv()

    for mask in range(1, cells):
        coef_copy(mask, flip(c, mask)).wait_recv()

    opposite_cell = flip(c, cells - 1)
    other_cell = jnp.bitwise_and(jnp.bitwise_xor(c, plan[0] + plan[1] - (cells - 1)), cells - 1)
    for at, guest in ((0, opposite_cell), (2, other_cell)):
        more, most = terms(guests[guest], coefs[guest])
        outbox[at : at + 1, :] = more
        outbox[at + 1 : at + 2, :] = most
    outbox[4:8, :] = jnp.zeros((4, share), jnp.float32)
    for mask in range(1, cells):
        result_copy(mask, c).start()

    @functools.partial(loop, own_steps)
    def _(j):
        for r in range(4):
            guest_copy(r, 2 * j + z % 2, c).wait_send()
        for r in range(1, 4):
            pass_copy(r, j, flip(c, relations[r])).wait_send()

    for mask in range(1, cells):
        coef_copy(mask, c).wait_send()
    for mask in range(1, cells):
        result_copy(mask, flip(c, mask)).wait_recv()
    first, second = results[opposite_cell], results[other_cell]
    total = total + first[0:1] + second[2:3]
    top = jnp.maximum(jnp.maximum(top, first[1:2]), second[3:4])
    qlive = z * share + lax.broadcasted_iota(jnp.int32, (1, share), 1) < fill
    density[...] = jnp.where(qlive, jnp.log(total), 0.0)
    spread[...] = jnp.where(qlive, jnp.sqrt(top / comps), 0.0)
    for mask in range(1, cells):
        result_copy(mask, c).wait_send()


def by_kernel(counts, loadings, kernel_widths, width_index, block_fill, plan):
    cells, groups = lax.axis_size("cell"), lax.axis_size("gene")
    rows, comps = counts.shape[0], loadings.shape[1]
    share = rows // groups
    steps, own_steps = rows // 2 // PIECE, share // PIECE
    block = pltpu.VMEM((rows, comps), jnp.bfloat16)
    dma = pltpu.SemaphoreType.DMA
    vmem = pl.BlockSpec(memory_space=pltpu.VMEM)
    out = jax.ShapeDtypeStruct((1, share), jnp.float32)
    density, spread = pl.pallas_call(
        functools.partial(kernel, cells),
        out_shape=(out, out),
        in_specs=[pl.BlockSpec(memory_space=pltpu.HBM)] * 6,
        out_specs=(vmem, vmem),
        scratch_shapes=[
            pltpu.VMEM(loadings.shape, loadings.dtype),
            pltpu.VMEM((1, share), width_index.dtype),
            pltpu.SMEM(kernel_widths.shape, kernel_widths.dtype),
            pltpu.SMEM(block_fill.shape, block_fill.dtype),
            pltpu.SMEM(plan.shape, plan.dtype),
            dma((5,)),
            pltpu.VMEM(counts.shape, counts.dtype),
            block,
            block,
            block,
            block,
            pltpu.VMEM((cells, share, comps), jnp.bfloat16),
            pltpu.VMEM((cells, 8, share), jnp.float32),
            pltpu.VMEM((8, share), jnp.float32),
            pltpu.VMEM((cells, 8, share), jnp.float32),
            pltpu.VMEM((rows, 128), jnp.float32),
            pltpu.VMEM((rows, 128), jnp.float32),
            pltpu.VMEM((comps, share), jnp.bfloat16),
            pltpu.VMEM((TILE, share), jnp.float32),
            pltpu.VMEM((TILE, share), jnp.float32),
            dma((2 * steps,)),
            dma((2 * steps,)),
            dma((2 * steps,)),
            dma((steps,)),
            dma((steps,)),
            dma((2 * steps,)),
            dma((2 * steps,)),
            dma((steps,)),
            dma((steps,)),
            dma((4 * own_steps,)),
            dma((4 * own_steps,)),
            dma((3 * own_steps,)),
            dma((3 * own_steps,)),
            dma((cells - 1,)),
            dma((cells - 1,)),
            dma((cells - 1,)),
            dma((cells - 1,)),
        ],
        compiler_params=pltpu.CompilerParams(
            collective_id=0, has_side_effects=True, vmem_limit_bytes=63 * 1024 * 1024
        ),
    )(counts, loadings, width_index.reshape(1, share), kernel_widths, block_fill, plan)
    return density.reshape(share), spread.reshape(share)


def exchange(value, stride, axis):
    cells = lax.axis_size(axis)
    for bit in range(cells.bit_length() - 1):
        pairs = [(source, source ^ (1 << bit)) for source in range(cells)]
        chosen = jnp.bitwise_and(jnp.right_shift(stride, bit), 1) == 1
        value = lax.cond(
            chosen,
            lambda v: jax.tree.map(lambda a: lax.ppermute(a, axis, pairs), v),
            lambda v: v,
            value,
        )
    return value


def block_terms(queries, coef, keys, fill):
    qf = queries.astype(jnp.float32)
    kf = keys.astype(jnp.float32)
    qnorm = jnp.sum(qf * qf, axis=1)
    knorm = jnp.sum(kf * kf, axis=1)
    inner = jnp.einsum("qc,kc->qk", queries, keys, preferred_element_type=jnp.float32)
    dist = jnp.maximum(qnorm[:, None] + knorm[None, :] - 2.0 * inner, 0.0)
    live = jnp.arange(keys.shape[0], dtype=jnp.int32)[None, :] < fill
    kernel = jnp.where(live, jnp.exp(-dist * coef[:, None]), 0.0)
    return (jnp.sum(kernel, axis=1), jnp.max(jnp.where(live, dist, 0.0), axis=1))


def lookup(table, index):
    slots = jnp.arange(table.shape[0], dtype=jnp.int32)
    return jnp.sum(jnp.where(slots == index, table, 0))


def by_exchange(counts, loadings, kernel_widths, width_index, block_fill, plan):
    groups = lax.axis_size("gene")
    share = counts.shape[0] // groups
    gene_pos = lax.axis_index("gene")
    own_fill = lookup(block_fill, lax.axis_index("cell"))
    partial_scores = jnp.dot(counts, loadings, preferred_element_type=jnp.float32)
    mine = lax.psum_scatter(partial_scores, "gene", scatter_dimension=0, tiled=True)
    mine = mine.astype(jnp.bfloat16)
    whole = lax.all_gather(mine, "gene", axis=0, tiled=True)
    comps = whole.shape[1]
    picked = width_index[:, None] == jnp.arange(kernel_widths.shape[0], dtype=jnp.int32)[None, :]
    width = jnp.sum(jnp.where(picked, kernel_widths[None, :], 0.0), axis=1)
    coef = 1.0 / (2.0 * comps * width * width)
    total, top = block_terms(mine, coef, whole, own_fill)
    for step in range(plan.shape[0]):
        guests, guest_coef = exchange((mine, coef), plan[step], "cell")
        terms = block_terms(guests, guest_coef, whole, own_fill)
        more, far = exchange(terms, plan[step], "cell")
        total = total + more
        top = jnp.maximum(top, far)
    positions = gene_pos * share + jnp.arange(share, dtype=jnp.int32)
    qlive = positions < own_fill
    density = jnp.where(qlive, jnp.log(total), 0.0)
    spread = jnp.where(qlive, jnp.sqrt(top / comps), 0.0)
    return (density, spread)


def solution(mesh):
    placed = (P("cell", "gene"), P("gene", None), P(), P(("cell", "gene")), P(), P())
    small = mesh.shape["cell"] == 8 and mesh.shape["gene"] == 4
    return jax.shard_map(
        by_kernel if small else by_exchange,
        mesh=mesh,
        in_specs=placed,
        out_specs=(P(("cell", "gene")), P(("cell", "gene"))),
        check_vma=False,
    )
```

```python
import functools
import math
import jax
import jax.numpy as jnp
from jax import lax
from jax.experimental import pallas as pl
from jax.experimental.pallas import tpu as pltpu
from jax.sharding import PartitionSpec as P

MESH = pl.DeviceIdType.MESH
PIECE = 128
TILE = 256
FAR = 1e30


def flip(place, mask):
    for bit in range(mask.bit_length()):
        if (mask >> bit) & 1:
            place = place + (1 << bit) * (1 - 2 * (place // (1 << bit) % 2))
    return place


def remote(src, dst, send, recv, **device):
    return pltpu.make_async_remote_copy(
        src_ref=src, dst_ref=dst, send_sem=send, recv_sem=recv, device_id=device, device_id_type=MESH
    )


def kernel(
    masks,
    counts,
    loadings_in,
    index_in,
    widths_in,
    fills_in,
    density,
    spread,
    loadings,
    index,
    widths,
    fills,
    small_sem,
    held,
    wire,
    inbox,
    cross,
    whole,
    guests,
    coefs,
    outbox,
    results,
    near_norm,
    far_norm,
    turned_queries,
    even,
    odd,
    held_sem,
    end_send,
    end_recv,
    mid_send,
    mid_recv,
    final_send,
    final_recv,
    over_send,
    over_recv,
    guest_send,
    guest_recv,
    coef_send,
    coef_recv,
    result_send,
    result_recv,
):
    c, z = lax.axis_index("cell"), lax.axis_index("gene")
    rows, comps = whole.shape
    half = rows // 2
    steps = half // PIECE
    share = guests.shape[1]
    own_steps = share // PIECE
    side = z // 2
    is_mid = (z + 1) // 2 % 2 == 1
    is_end = (z + 1) // 2 % 2 == 0
    mate = z + 1 - 2 * (z % 2)
    opposite = 3 - z
    near, far = side * half, half - side * half

    def part(base, i):
        return piece(base, i % 2 * own_steps + i // 2)

    def piece(base, i):
        return pl.ds(pl.multiple_of(base + i * PIECE, PIECE), PIECE)

    def held_copy(base, i, k):
        at = part(base, i)
        return pltpu.make_async_copy(counts.at[at], held.at[at], held_sem.at[2 * i + k])

    def end_copy(base, i, k):
        at = part(base, i)
        return remote(wire.at[at], inbox.at[at], end_send.at[2 * i + k], end_recv.at[2 * i + k], gene=mate)

    def mid_copy(base, i):
        at = part(base, i)
        return remote(wire.at[at], cross.at[at], mid_send.at[i], mid_recv.at[i], gene=opposite)

    def final_copy(base, i, k):
        at = part(base, i)
        return remote(whole.at[at], whole.at[at], final_send.at[2 * i + k], final_recv.at[2 * i + k], gene=mate)

    def over_copy(base, i):
        at = part(base, i)
        return remote(whole.at[at], whole.at[at], over_send.at[i], over_recv.at[i], gene=opposite)

    def guest_copy(r, i):
        j = i // 2
        return remote(
            whole.at[part(near, i)],
            guests.at[r, piece(0, j)],
            guest_send.at[r * own_steps + j],
            guest_recv.at[r * own_steps + j],
            cell=flip(c, masks[r]),
        )

    def coef_copy(r):
        return remote(coefs.at[2], coefs.at[r], coef_send.at[r], coef_recv.at[r], cell=flip(c, masks[r]))

    def result_copy(r):
        return remote(outbox.at[r], results.at[r], result_send.at[r], result_recv.at[r], cell=flip(c, masks[r]))

    def offer(i):
        @pl.when(i % 2 == z % 2)
        def _():
            for r in range(2):
                guest_copy(r, i).start()

    def product(base, i, k):
        held_copy(base, i, k).wait()
        return jnp.dot(held[part(base, i), :], loadings[...], preferred_element_type=jnp.float32)

    def norms(base, i):
        at = part(base, i)
        keys = whole[at, :].astype(jnp.float32)
        norm = jnp.sum(keys * keys, axis=1, keepdims=True)
        first = base + (i % 2 * own_steps + i // 2) * PIECE
        live = first + lax.broadcasted_iota(jnp.int32, (PIECE, 1), 0) < fill
        near_norm[at, :] = jnp.broadcast_to(jnp.where(live, norm, FAR), (PIECE, 128))
        far_norm[at, :] = jnp.broadcast_to(jnp.where(live, norm, -FAR), (PIECE, 128))

    def loop(count, body):
        def step(i, carry):
            body(i)
            return carry

        lax.fori_loop(0, count, step, 0)

    small = [
        pltpu.make_async_copy(source, target, small_sem.at[k])
        for k, (source, target) in enumerate(
            (
                (loadings_in, loadings),
                (index_in, index),
                (widths_in, widths),
                (fills_in, fills),
            )
        )
    ]
    small[0].start()
    held_copy(far, 0, 0).start()
    held_copy(near, 0, 1).start()
    for copy in small[1:]:
        copy.start()

    @functools.partial(loop, steps - 1)
    def _(i):
        held_copy(far, i + 1, 0).start()
        held_copy(near, i + 1, 1).start()

    barrier = pltpu.get_barrier_semaphore()
    for mask in masks:
        pl.semaphore_signal(barrier, inc=1, device_id={"cell": flip(c, mask)}, device_id_type=MESH)
    pl.semaphore_signal(barrier, inc=1, device_id={"gene": mate}, device_id_type=MESH)

    @pl.when(is_mid)
    def _():
        pl.semaphore_signal(barrier, inc=1, device_id={"gene": opposite}, device_id_type=MESH)

    for copy in small:
        copy.wait()
    fill = fills[c]
    picked = jnp.zeros(index.shape, jnp.float32)
    for entry in range(widths.shape[0]):
        picked = picked + jnp.where(index[...] == entry, widths[entry], 0.0)
    own_coef = 1.0 / (2.0 * comps * picked * picked)
    coefs[2] = jnp.broadcast_to(own_coef, (8, share))

    @pl.when(is_end)
    def _():
        pl.semaphore_wait(barrier, 3)

        @functools.partial(loop, steps)
        def _(i):
            for k, base in enumerate((far, near)):
                wire[part(base, i), :] = product(base, i, k).astype(wire.dtype)
                end_copy(base, i, k).start()

        for r in range(2):
            coef_copy(r).start()

        @functools.partial(loop, steps)
        def _(i):
            final_copy(near, i, 1).wait_recv()
            offer(i)
            norms(near, i)
            final_copy(far, i, 0).wait_recv()
            norms(far, i)

        @functools.partial(loop, steps)
        def _(i):
            end_copy(far, i, 0).wait_send()
            end_copy(near, i, 1).wait_send()

    @pl.when(is_mid)
    def _():
        pl.semaphore_wait(barrier, 4)
        for r in range(2):
            coef_copy(r).start()

        @functools.partial(loop, steps + 2)
        def _(i):
            @pl.when(i < steps)
            def _():
                total = product(far, i, 0)
                end_copy(far, i, 0).wait_recv()
                total = total + inbox[part(far, i), :].astype(jnp.float32)
                wire[part(far, i), :] = total.astype(wire.dtype)
                mid_copy(far, i).start()

            @pl.when(i >= 2)
            def _():
                over_copy(far, i - 2).wait_recv()
                final_copy(far, i - 2, 0).start()
                norms(far, i - 2)

            @pl.when((i >= 1) & (i <= steps))
            def _():
                total = product(near, i - 1, 1)
                end_copy(near, i - 1, 1).wait_recv()
                total = total + inbox[part(near, i - 1), :].astype(jnp.float32)
                mid_copy(near, i - 1).wait_recv()
                total = total + cross[part(near, i - 1), :].astype(jnp.float32)
                whole[part(near, i - 1), :] = total.astype(whole.dtype)
                over_copy(near, i - 1).start()
                final_copy(near, i - 1, 1).start()
                offer(i - 1)
                norms(near, i - 1)

        @functools.partial(loop, steps)
        def _(i):
            mid_copy(far, i).wait_send()
            over_copy(near, i).wait_send()
            final_copy(near, i, 1).wait_send()
            final_copy(far, i, 0).wait_send()

    def terms(queries, coef):
        turned = queries.astype(jnp.float32).T
        norm = jnp.broadcast_to(jnp.sum(turned * turned, axis=0, keepdims=True), (8, share))
        turned_queries[...] = (turned * -2.0).astype(turned_queries.dtype)
        rate = coef * (-1.0 / math.log(2.0))
        tiles = rows // TILE

        def multiply(t, target):
            at = pl.ds(pl.multiple_of(t * TILE, TILE), TILE)
            target[...] = jnp.dot(whole[at, :], turned_queries[...], preferred_element_type=jnp.float32)

        def collect(t, source, total, top):
            for group in range(TILE // 8):
                at = pl.ds(pl.multiple_of(t * TILE + group * 8, 8), 8)
                base = source[group * 8 : group * 8 + 8, :] + norm
                closest = jnp.concatenate([near_norm[at, :]] * (share // 128), axis=1)
                farthest = jnp.concatenate([far_norm[at, :]] * (share // 128), axis=1)
                total = total + jnp.exp2(jnp.maximum(base + closest, 0.0) * rate)
                top = jnp.maximum(top, base + farthest)
            return total, top

        def step(t, carry):
            total, top = carry
            multiply(2 * t + 1, odd)
            total, top = collect(2 * t, even, total, top)
            multiply(jnp.minimum(2 * t + 2, tiles - 1), even)
            return collect(2 * t + 1, odd, total, top)

        zero = jnp.zeros((8, share), jnp.float32)
        multiply(0, even)
        total, top = lax.fori_loop(0, tiles // 2, step, (zero, zero))
        return jnp.sum(total, axis=0, keepdims=True), jnp.max(top, axis=0, keepdims=True)

    own_rows = pl.ds(pl.multiple_of(z * share, share), share)
    total, top = terms(whole[own_rows, :], coefs[2])
    for r in (1, 0):

        @functools.partial(loop, own_steps)
        def _(j):
            guest_copy(r, 2 * j + z % 2).wait_recv()

        coef_copy(r).wait_recv()
        more, most = terms(guests[r], coefs[r])
        outbox[r] = jnp.concatenate([more, most, jnp.zeros((6, share), jnp.float32)], axis=0)
        result_copy(r).start()

    @functools.partial(loop, own_steps)
    def _(j):
        for r in range(2):
            guest_copy(r, 2 * j + z % 2).wait_send()

    for r in (1, 0):
        coef_copy(r).wait_send()
        result_copy(r).wait_recv()
        back = results[r]
        total = total + back[0:1]
        top = jnp.maximum(top, back[1:2])
    qlive = z * share + lax.broadcasted_iota(jnp.int32, (1, share), 1) < fill
    density[...] = jnp.where(qlive, jnp.log(total), 0.0)
    spread[...] = jnp.where(qlive, jnp.sqrt(top / comps), 0.0)
    for r in range(2):
        result_copy(r).wait_send()


def by_kernel(counts, loadings, kernel_widths, width_index, block_fill, plan):
    cells, groups = lax.axis_size("cell"), lax.axis_size("gene")
    rows, comps = counts.shape[0], loadings.shape[1]
    share = rows // groups
    steps, own_steps = rows // 2 // PIECE, share // PIECE
    block = pltpu.VMEM((rows, comps), jnp.bfloat16)
    dma = pltpu.SemaphoreType.DMA
    vmem = pl.BlockSpec(memory_space=pltpu.VMEM)
    out = jax.ShapeDtypeStruct((1, share), jnp.float32)

    def call(other):
        return pl.pallas_call(
            functools.partial(kernel, (cells - 1, other)),
            out_shape=(out, out),
            in_specs=[pl.BlockSpec(memory_space=pltpu.HBM)] * 5,
            out_specs=(vmem, vmem),
            scratch_shapes=[
                pltpu.VMEM(loadings.shape, loadings.dtype),
                pltpu.VMEM((1, share), width_index.dtype),
                pltpu.SMEM(kernel_widths.shape, kernel_widths.dtype),
                pltpu.SMEM(block_fill.shape, block_fill.dtype),
                dma((4,)),
                pltpu.VMEM(counts.shape, counts.dtype),
                block,
                block,
                block,
                block,
                pltpu.VMEM((2, share, comps), jnp.bfloat16),
                pltpu.VMEM((3, 8, share), jnp.float32),
                pltpu.VMEM((2, 8, share), jnp.float32),
                pltpu.VMEM((2, 8, share), jnp.float32),
                pltpu.VMEM((rows, 128), jnp.float32),
                pltpu.VMEM((rows, 128), jnp.float32),
                pltpu.VMEM((comps, share), jnp.bfloat16),
                pltpu.VMEM((TILE, share), jnp.float32),
                pltpu.VMEM((TILE, share), jnp.float32),
                dma((2 * steps,)),
                dma((2 * steps,)),
                dma((2 * steps,)),
                dma((steps,)),
                dma((steps,)),
                dma((2 * steps,)),
                dma((2 * steps,)),
                dma((steps,)),
                dma((steps,)),
                dma((2 * own_steps,)),
                dma((2 * own_steps,)),
                dma((2,)),
                dma((2,)),
                dma((2,)),
                dma((2,)),
            ],
            compiler_params=pltpu.CompilerParams(
                collective_id=other - 1, has_side_effects=True, vmem_limit_bytes=63 * 1024 * 1024
            ),
        )

    arrays = (counts, loadings, width_index.reshape(1, share), kernel_widths, block_fill)
    other = plan[0] + plan[1] - (cells - 1)
    density, spread = lax.switch(other - 1, [call(mask) for mask in range(1, cells - 1)], *arrays)
    return density.reshape(share), spread.reshape(share)


def exchange(value, stride, axis):
    cells = lax.axis_size(axis)
    for bit in range(cells.bit_length() - 1):
        pairs = [(source, source ^ (1 << bit)) for source in range(cells)]
        chosen = jnp.bitwise_and(jnp.right_shift(stride, bit), 1) == 1
        value = lax.cond(
            chosen,
            lambda v: jax.tree.map(lambda a: lax.ppermute(a, axis, pairs), v),
            lambda v: v,
            value,
        )
    return value


def block_terms(queries, coef, keys, fill):
    qf = queries.astype(jnp.float32)
    kf = keys.astype(jnp.float32)
    qnorm = jnp.sum(qf * qf, axis=1)
    knorm = jnp.sum(kf * kf, axis=1)
    inner = jnp.einsum("qc,kc->qk", queries, keys, preferred_element_type=jnp.float32)
    dist = jnp.maximum(qnorm[:, None] + knorm[None, :] - 2.0 * inner, 0.0)
    live = jnp.arange(keys.shape[0], dtype=jnp.int32)[None, :] < fill
    kernel = jnp.where(live, jnp.exp(-dist * coef[:, None]), 0.0)
    return (jnp.sum(kernel, axis=1), jnp.max(jnp.where(live, dist, 0.0), axis=1))


def lookup(table, index):
    slots = jnp.arange(table.shape[0], dtype=jnp.int32)
    return jnp.sum(jnp.where(slots == index, table, 0))


def by_exchange(counts, loadings, kernel_widths, width_index, block_fill, plan):
    groups = lax.axis_size("gene")
    share = counts.shape[0] // groups
    gene_pos = lax.axis_index("gene")
    own_fill = lookup(block_fill, lax.axis_index("cell"))
    partial_scores = jnp.dot(counts, loadings, preferred_element_type=jnp.float32)
    mine = lax.psum_scatter(partial_scores, "gene", scatter_dimension=0, tiled=True)
    mine = mine.astype(jnp.bfloat16)
    whole = lax.all_gather(mine, "gene", axis=0, tiled=True)
    comps = whole.shape[1]
    picked = width_index[:, None] == jnp.arange(kernel_widths.shape[0], dtype=jnp.int32)[None, :]
    width = jnp.sum(jnp.where(picked, kernel_widths[None, :], 0.0), axis=1)
    coef = 1.0 / (2.0 * comps * width * width)
    total, top = block_terms(mine, coef, whole, own_fill)
    for step in range(plan.shape[0]):
        guests, guest_coef = exchange((mine, coef), plan[step], "cell")
        terms = block_terms(guests, guest_coef, whole, own_fill)
        more, far = exchange(terms, plan[step], "cell")
        total = total + more
        top = jnp.maximum(top, far)
    positions = gene_pos * share + jnp.arange(share, dtype=jnp.int32)
    qlive = positions < own_fill
    density = jnp.where(qlive, jnp.log(total), 0.0)
    spread = jnp.where(qlive, jnp.sqrt(top / comps), 0.0)
    return (density, spread)


def solution(mesh):
    placed = (P("cell", "gene"), P("gene", None), P(), P(("cell", "gene")), P(), P())
    small = mesh.shape["cell"] == 8 and mesh.shape["gene"] == 4
    return jax.shard_map(
        by_kernel if small else by_exchange,
        mesh=mesh,
        in_specs=placed,
        out_specs=(P(("cell", "gene")), P(("cell", "gene"))),
        check_vma=False,
    )
```

```python
import functools
import math
import jax
import jax.numpy as jnp
from jax import lax
from jax.experimental import pallas as pl
from jax.experimental.pallas import tpu as pltpu
from jax.sharding import PartitionSpec as P

MESH = pl.DeviceIdType.MESH
PIECE = 256
TILE = 256
FAR = 1e30


def flip(place, mask):
    for bit in range(mask.bit_length()):
        if (mask >> bit) & 1:
            place = place + (1 << bit) * (1 - 2 * (place // (1 << bit) % 2))
    return place


def remote(src, dst, send, recv, **device):
    return pltpu.make_async_remote_copy(
        src_ref=src, dst_ref=dst, send_sem=send, recv_sem=recv, device_id=device, device_id_type=MESH
    )


def kernel(
    cells,
    counts,
    loadings_in,
    index_in,
    widths_in,
    fills_in,
    plan_in,
    density,
    spread,
    loadings,
    index,
    widths,
    fills,
    plan,
    small_sem,
    held,
    wire,
    inbox,
    cross,
    whole,
    guests,
    coefs,
    outbox,
    results,
    near_norm,
    far_norm,
    turned_queries,
    even,
    odd,
    held_sem,
    end_send,
    end_recv,
    mid_send,
    mid_recv,
    final_send,
    final_recv,
    over_send,
    over_recv,
    guest_send,
    guest_recv,
    pass_send,
    pass_recv,
    coef_send,
    coef_recv,
    result_send,
    result_recv,
):
    c, z = lax.axis_index("cell"), lax.axis_index("gene")
    rows, comps = whole.shape
    half = rows // 2
    steps = half // PIECE
    share = guests.shape[1]
    own_steps = share // PIECE
    side = z // 2
    is_mid = (z + 1) // 2 % 2 == 1
    is_end = (z + 1) // 2 % 2 == 0
    mate = z + 1 - 2 * (z % 2)
    opposite = 3 - z
    near, far = side * half, half - side * half
    relations = (1, 2, 4, 6)

    def part(base, i):
        return piece(base, i % 2 * own_steps + i // 2)

    def piece(base, i):
        return pl.ds(pl.multiple_of(base + i * PIECE, PIECE), PIECE)

    def held_copy(base, i, k):
        at = part(base, i)
        return pltpu.make_async_copy(counts.at[at], held.at[at], held_sem.at[2 * i + k])

    def end_copy(base, i, k):
        at = part(base, i)
        return remote(wire.at[at], inbox.at[at], end_send.at[2 * i + k], end_recv.at[2 * i + k], gene=mate)

    def mid_copy(base, i):
        at = part(base, i)
        return remote(wire.at[at], cross.at[at], mid_send.at[i], mid_recv.at[i], gene=opposite)

    def final_copy(base, i, k):
        at = part(base, i)
        return remote(whole.at[at], whole.at[at], final_send.at[2 * i + k], final_recv.at[2 * i + k], gene=mate)

    def over_copy(base, i):
        at = part(base, i)
        return remote(whole.at[at], whole.at[at], over_send.at[i], over_recv.at[i], gene=opposite)

    def guest_copy(r, i, slot):
        j = i // 2
        return remote(
            whole.at[part(near, i)],
            guests.at[slot, piece(0, j)],
            guest_send.at[r * own_steps + j],
            guest_recv.at[r * own_steps + j],
            cell=flip(c, relations[r]),
        )

    def pass_copy(r, j, slot):
        at = piece(0, j)
        return remote(
            guests.at[slot, at],
            guests.at[slot, at],
            pass_send.at[(r - 1) * own_steps + j],
            pass_recv.at[(r - 1) * own_steps + j],
            cell=flip(c, 1),
        )

    def coef_copy(mask, slot):
        return remote(
            coefs.at[slot], coefs.at[slot], coef_send.at[mask - 1], coef_recv.at[mask - 1], cell=flip(c, mask)
        )

    def result_copy(mask, slot):
        return remote(
            outbox, results.at[slot], result_send.at[mask - 1], result_recv.at[mask - 1], cell=flip(c, mask)
        )

    def offer(i):
        @pl.when(i % 2 == z % 2)
        def _():
            for r in range(4):
                guest_copy(r, i, c).start()

    def product(base, i, k):
        held_copy(base, i, k).wait()
        return jnp.dot(held[part(base, i), :], loadings[...], preferred_element_type=jnp.float32)

    def norms(base, i):
        at = part(base, i)
        keys = whole[at, :].astype(jnp.float32)
        norm = jnp.sum(keys * keys, axis=1, keepdims=True)
        first = base + (i % 2 * own_steps + i // 2) * PIECE
        live = first + lax.broadcasted_iota(jnp.int32, (PIECE, 1), 0) < fill
        near_norm[at, :] = jnp.broadcast_to(jnp.where(live, norm, FAR), (PIECE, 128))
        far_norm[at, :] = jnp.broadcast_to(jnp.where(live, norm, -FAR), (PIECE, 128))

    def loop(count, body):
        def step(i, carry):
            body(i)
            return carry

        lax.fori_loop(0, count, step, 0)

    small = [
        pltpu.make_async_copy(source, target, small_sem.at[k])
        for k, (source, target) in enumerate(
            (
                (loadings_in, loadings),
                (index_in, index),
                (widths_in, widths),
                (fills_in, fills),
                (plan_in, plan),
            )
        )
    ]
    small[0].start()
    held_copy(far, 0, 0).start()
    held_copy(near, 0, 1).start()
    for copy in small[1:]:
        copy.start()

    @functools.partial(loop, steps - 1)
    def _(i):
        held_copy(far, i + 1, 0).start()
        held_copy(near, i + 1, 1).start()

    barrier = pltpu.get_barrier_semaphore()
    for mask in range(1, cells):
        pl.semaphore_signal(barrier, inc=1, device_id={"cell": flip(c, mask)}, device_id_type=MESH)
    pl.semaphore_signal(barrier, inc=1, device_id={"gene": mate}, device_id_type=MESH)

    @pl.when(is_mid)
    def _():
        pl.semaphore_signal(barrier, inc=1, device_id={"gene": opposite}, device_id_type=MESH)

    for copy in small:
        copy.wait()
    fill = fills[c]
    picked = jnp.zeros(index.shape, jnp.float32)
    for entry in range(widths.shape[0]):
        picked = picked + jnp.where(index[...] == entry, widths[entry], 0.0)
    own_coef = 1.0 / (2.0 * comps * picked * picked)
    coefs[c] = jnp.broadcast_to(own_coef, (8, share))

    @pl.when(is_end)
    def _():
        pl.semaphore_wait(barrier, cells)

        @functools.partial(loop, steps)
        def _(i):
            for k, base in enumerate((far, near)):
                wire[part(base, i), :] = product(base, i, k).astype(wire.dtype)
                end_copy(base, i, k).start()

        for mask in range(1, cells):
            coef_copy(mask, c).start()

        @functools.partial(loop, steps)
        def _(i):
            final_copy(near, i, 1).wait_recv()
            offer(i)
            norms(near, i)
            final_copy(far, i, 0).wait_recv()
            norms(far, i)

        @functools.partial(loop, steps)
        def _(i):
            end_copy(far, i, 0).wait_send()
            end_copy(near, i, 1).wait_send()

    @pl.when(is_mid)
    def _():
        pl.semaphore_wait(barrier, cells + 1)
        for mask in range(1, cells):
            coef_copy(mask, c).start()

        @functools.partial(loop, steps + 2)
        def _(i):
            @pl.when(i < steps)
            def _():
                total = product(far, i, 0)
                end_copy(far, i, 0).wait_recv()
                total = total + inbox[part(far, i), :].astype(jnp.float32)
                wire[part(far, i), :] = total.astype(wire.dtype)
                mid_copy(far, i).start()

            @pl.when(i >= 2)
            def _():
                over_copy(far, i - 2).wait_recv()
                final_copy(far, i - 2, 0).start()
                norms(far, i - 2)

            @pl.when((i >= 1) & (i <= steps))
            def _():
                total = product(near, i - 1, 1)
                end_copy(near, i - 1, 1).wait_recv()
                total = total + inbox[part(near, i - 1), :].astype(jnp.float32)
                mid_copy(near, i - 1).wait_recv()
                total = total + cross[part(near, i - 1), :].astype(jnp.float32)
                whole[part(near, i - 1), :] = total.astype(whole.dtype)
                over_copy(near, i - 1).start()
                final_copy(near, i - 1, 1).start()
                offer(i - 1)
                norms(near, i - 1)

        @functools.partial(loop, steps)
        def _(i):
            mid_copy(far, i).wait_send()
            over_copy(near, i).wait_send()
            final_copy(near, i, 1).wait_send()
            final_copy(far, i, 0).wait_send()

    def forward(j):
        for r in range(1, 4):
            slot = flip(c, relations[r])
            guest_copy(r, 2 * j + z % 2, slot).wait_recv()
            pass_copy(r, j, slot).start()

    loop(own_steps - 1, forward)

    def terms(queries, coef):
        turned = queries.astype(jnp.float32).T
        norm = jnp.broadcast_to(jnp.sum(turned * turned, axis=0, keepdims=True), (8, share))
        turned_queries[...] = (turned * -2.0).astype(turned_queries.dtype)
        rate = coef * (-1.0 / math.log(2.0))
        tiles = rows // TILE

        def multiply(t, target):
            at = pl.ds(pl.multiple_of(t * TILE, TILE), TILE)
            target[...] = jnp.dot(whole[at, :], turned_queries[...], preferred_element_type=jnp.float32)

        def collect(t, source, total, top):
            for group in range(TILE // 8):
                at = pl.ds(pl.multiple_of(t * TILE + group * 8, 8), 8)
                base = source[group * 8 : group * 8 + 8, :] + norm
                closest = jnp.concatenate([near_norm[at, :]] * (share // 128), axis=1)
                farthest = jnp.concatenate([far_norm[at, :]] * (share // 128), axis=1)
                total = total + jnp.exp2(jnp.maximum(base + closest, 0.0) * rate)
                top = jnp.maximum(top, base + farthest)
            return total, top

        def step(t, carry):
            total, top = carry
            multiply(2 * t + 1, odd)
            total, top = collect(2 * t, even, total, top)
            multiply(jnp.minimum(2 * t + 2, tiles - 1), even)
            return collect(2 * t + 1, odd, total, top)

        zero = jnp.zeros((8, share), jnp.float32)
        multiply(0, even)
        total, top = lax.fori_loop(0, tiles // 2, step, (zero, zero))
        return jnp.sum(total, axis=0, keepdims=True), jnp.max(top, axis=0, keepdims=True)

    own_rows = pl.ds(pl.multiple_of(z * share, share), share)
    total, top = terms(whole[own_rows, :], coefs[c])
    forward(own_steps - 1)

    @functools.partial(loop, own_steps)
    def _(j):
        guest_copy(0, 2 * j + z % 2, flip(c, 1)).wait_recv()
        for r in range(1, 4):
            pass_copy(r, j, flip(c, relations[r] + 1)).wait_recv()

    for mask in range(1, cells):
        coef_copy(mask, flip(c, mask)).wait_recv()

    opposite_cell = flip(c, cells - 1)
    other_cell = jnp.bitwise_and(jnp.bitwise_xor(c, plan[0] + plan[1] - (cells - 1)), cells - 1)
    for at, guest in ((0, opposite_cell), (2, other_cell)):
        more, most = terms(guests[guest], coefs[guest])
        outbox[at : at + 1, :] = more
        outbox[at + 1 : at + 2, :] = most
    outbox[4:8, :] = jnp.zeros((4, share), jnp.float32)
    for mask in range(1, cells):
        result_copy(mask, c).start()

    @functools.partial(loop, own_steps)
    def _(j):
        for r in range(4):
            guest_copy(r, 2 * j + z % 2, c).wait_send()
        for r in range(1, 4):
            pass_copy(r, j, flip(c, relations[r])).wait_send()

    for mask in range(1, cells):
        coef_copy(mask, c).wait_send()
    for mask in range(1, cells):
        result_copy(mask, flip(c, mask)).wait_recv()
    first, second = results[opposite_cell], results[other_cell]
    total = total + first[0:1] + second[2:3]
    top = jnp.maximum(jnp.maximum(top, first[1:2]), second[3:4])
    qlive = z * share + lax.broadcasted_iota(jnp.int32, (1, share), 1) < fill
    density[...] = jnp.where(qlive, jnp.log(total), 0.0)
    spread[...] = jnp.where(qlive, jnp.sqrt(top / comps), 0.0)
    for mask in range(1, cells):
        result_copy(mask, c).wait_send()


def by_kernel(counts, loadings, kernel_widths, width_index, block_fill, plan):
    cells, groups = lax.axis_size("cell"), lax.axis_size("gene")
    rows, comps = counts.shape[0], loadings.shape[1]
    share = rows // groups
    steps, own_steps = rows // 2 // PIECE, share // PIECE
    block = pltpu.VMEM((rows, comps), jnp.bfloat16)
    dma = pltpu.SemaphoreType.DMA
    vmem = pl.BlockSpec(memory_space=pltpu.VMEM)
    out = jax.ShapeDtypeStruct((1, share), jnp.float32)
    density, spread = pl.pallas_call(
        functools.partial(kernel, cells),
        out_shape=(out, out),
        in_specs=[pl.BlockSpec(memory_space=pltpu.HBM)] * 6,
        out_specs=(vmem, vmem),
        scratch_shapes=[
            pltpu.VMEM(loadings.shape, loadings.dtype),
            pltpu.VMEM((1, share), width_index.dtype),
            pltpu.SMEM(kernel_widths.shape, kernel_widths.dtype),
            pltpu.SMEM(block_fill.shape, block_fill.dtype),
            pltpu.SMEM(plan.shape, plan.dtype),
            dma((5,)),
            pltpu.VMEM(counts.shape, counts.dtype),
            block,
            block,
            block,
            block,
            pltpu.VMEM((cells, share, comps), jnp.bfloat16),
            pltpu.VMEM((cells, 8, share), jnp.float32),
            pltpu.VMEM((8, share), jnp.float32),
            pltpu.VMEM((cells, 8, share), jnp.float32),
            pltpu.VMEM((rows, 128), jnp.float32),
            pltpu.VMEM((rows, 128), jnp.float32),
            pltpu.VMEM((comps, share), jnp.bfloat16),
            pltpu.VMEM((TILE, share), jnp.float32),
            pltpu.VMEM((TILE, share), jnp.float32),
            dma((2 * steps,)),
            dma((2 * steps,)),
            dma((2 * steps,)),
            dma((steps,)),
            dma((steps,)),
            dma((2 * steps,)),
            dma((2 * steps,)),
            dma((steps,)),
            dma((steps,)),
            dma((4 * own_steps,)),
            dma((4 * own_steps,)),
            dma((3 * own_steps,)),
            dma((3 * own_steps,)),
            dma((cells - 1,)),
            dma((cells - 1,)),
            dma((cells - 1,)),
            dma((cells - 1,)),
        ],
        compiler_params=pltpu.CompilerParams(
            collective_id=0, has_side_effects=True, vmem_limit_bytes=63 * 1024 * 1024
        ),
    )(counts, loadings, width_index.reshape(1, share), kernel_widths, block_fill, plan)
    return density.reshape(share), spread.reshape(share)


def exchange(value, stride, axis):
    cells = lax.axis_size(axis)
    for bit in range(cells.bit_length() - 1):
        pairs = [(source, source ^ (1 << bit)) for source in range(cells)]
        chosen = jnp.bitwise_and(jnp.right_shift(stride, bit), 1) == 1
        value = lax.cond(
            chosen,
            lambda v: jax.tree.map(lambda a: lax.ppermute(a, axis, pairs), v),
            lambda v: v,
            value,
        )
    return value


def block_terms(queries, coef, keys, fill):
    qf = queries.astype(jnp.float32)
    kf = keys.astype(jnp.float32)
    qnorm = jnp.sum(qf * qf, axis=1)
    knorm = jnp.sum(kf * kf, axis=1)
    inner = jnp.einsum("qc,kc->qk", queries, keys, preferred_element_type=jnp.float32)
    dist = jnp.maximum(qnorm[:, None] + knorm[None, :] - 2.0 * inner, 0.0)
    live = jnp.arange(keys.shape[0], dtype=jnp.int32)[None, :] < fill
    kernel = jnp.where(live, jnp.exp(-dist * coef[:, None]), 0.0)
    return (jnp.sum(kernel, axis=1), jnp.max(jnp.where(live, dist, 0.0), axis=1))


def lookup(table, index):
    slots = jnp.arange(table.shape[0], dtype=jnp.int32)
    return jnp.sum(jnp.where(slots == index, table, 0))


def by_exchange(counts, loadings, kernel_widths, width_index, block_fill, plan):
    groups = lax.axis_size("gene")
    share = counts.shape[0] // groups
    gene_pos = lax.axis_index("gene")
    own_fill = lookup(block_fill, lax.axis_index("cell"))
    partial_scores = jnp.dot(counts, loadings, preferred_element_type=jnp.float32)
    mine = lax.psum_scatter(partial_scores, "gene", scatter_dimension=0, tiled=True)
    mine = mine.astype(jnp.bfloat16)
    whole = lax.all_gather(mine, "gene", axis=0, tiled=True)
    comps = whole.shape[1]
    picked = width_index[:, None] == jnp.arange(kernel_widths.shape[0], dtype=jnp.int32)[None, :]
    width = jnp.sum(jnp.where(picked, kernel_widths[None, :], 0.0), axis=1)
    coef = 1.0 / (2.0 * comps * width * width)
    total, top = block_terms(mine, coef, whole, own_fill)
    for step in range(plan.shape[0]):
        guests, guest_coef = exchange((mine, coef), plan[step], "cell")
        terms = block_terms(guests, guest_coef, whole, own_fill)
        more, far = exchange(terms, plan[step], "cell")
        total = total + more
        top = jnp.maximum(top, far)
    positions = gene_pos * share + jnp.arange(share, dtype=jnp.int32)
    qlive = positions < own_fill
    density = jnp.where(qlive, jnp.log(total), 0.0)
    spread = jnp.where(qlive, jnp.sqrt(top / comps), 0.0)
    return (density, spread)


def solution(mesh):
    placed = (P("cell", "gene"), P("gene", None), P(), P(("cell", "gene")), P(), P())
    small = mesh.shape["cell"] == 8 and mesh.shape["gene"] == 4
    return jax.shard_map(
        by_kernel if small else by_exchange,
        mesh=mesh,
        in_specs=placed,
        out_specs=(P(("cell", "gene")), P(("cell", "gene"))),
        check_vma=False,
    )
```
